512 devices in a mesh: grp: 16 (over y_lo, z), dev: 32 (over x, y_hi, core).
Axes of the slice: x: 4, y: 8 (y_hi: 4, y_lo: 2; y = y_hi * 2 + y_lo), z: 8, core: 2. Of those that a mesh axis runs over, the one named last changes fastest.
Arguments:
- samples: bfloat16 [262144, 768], P(('grp', 'dev')), may hold values from -8 to 8
- targets: bfloat16 [262144, 768], P(('grp', 'dev')), may hold values from -8 to 8
- row_slot: int32 [262144], P(('grp', 'dev')), may hold values from 0 to 63, as said below
- hot_group: int32 [32], P('dev'), may hold values from 0 to 15
- anchor: bfloat16 [512, 768, 768], P(('grp', 'dev')), may hold values from -0.21875 to 0.21875
Outputs:
- rotation: bfloat16 [512, 768, 768], P(('grp', 'dev'))
The draws below stay inside these ranges and needn't reach their ends.
Inputs may be any that keep to these rules, and one draw needn't show every extreme that they name: `row_slot`: on each device at most 16 rows carry the same value; in every group one value is carried by exactly 16 rows on every device of the group.
All inputs are finite; a program needn't handle non-finite values.
Results may differ from the reference program's by a relative error of at most 0.027.
Values may be sent and summed in bfloat16 or wider, within the bound.
A program may use at most 128 MiB of HBM per device.

```python
import math
import jax
import jax.numpy as jnp
from jax import lax

D = 768
ROWS_DEV = 512
ITERS = 2
LISTS = 512
ROWS = 262144
N_GRP = 16
N_DEV = 32


def draw_samples(key, part):
    key = jax.random.fold_in(key, 3)
    values = jnp.clip(jax.random.normal(key, (ROWS, D), jnp.float32), -8.0, 8.0)
    return values.astype(jnp.bfloat16)


def draw_targets(key, part):
    key = jax.random.fold_in(key, 7)
    values = jnp.clip(jax.random.normal(key, (ROWS, D), jnp.float32), -8.0, 8.0)
    return values.astype(jnp.bfloat16)


def draw_row_slot(key, part):
    key = jax.random.fold_in(key, 11)
    buckets = 2 * N_DEV
    capacity = ROWS_DEV // N_DEV
    spare_slots = (buckets - 1) * capacity
    full_key, favour_key, device_key = jax.random.split(key, 3)
    fullest = jax.random.randint(full_key, (N_GRP,), 0, buckets)
    favour = jax.random.randint(favour_key, (N_GRP, buckets), 0, 4 * ROWS_DEV)
    device_keys = jax.random.split(device_key, N_GRP * N_DEV)
    groups_of = jnp.arange(N_GRP * N_DEV, dtype=jnp.int32) // N_DEV

    def one_device(device_seed, group_index):
        jitter_key, order_key = jax.random.split(device_seed)
        slot_index = jnp.arange(spare_slots, dtype=jnp.int32)
        others = slot_index // capacity
        bucket_label = others + (others >= fullest[group_index]).astype(jnp.int32)
        jitter = jax.random.randint(jitter_key, (spare_slots,), 0, 4 * ROWS_DEV)
        ranking = (jitter + jnp.take(favour[group_index], bucket_label)) * spare_slots + slot_index
        picked = jnp.take(bucket_label, jnp.argsort(ranking)[:ROWS_DEV - capacity])
        row_labels = jnp.concatenate([jnp.full((capacity,), fullest[group_index], jnp.int32), picked])
        return jnp.take(row_labels, jax.random.permutation(order_key, ROWS_DEV))
    return jax.vmap(one_device)(device_keys, groups_of).reshape(-1).astype(jnp.int32)


def place_ends(drawn, rng, smallest, high):
    dims = drawn.shape
    place = [jax.random.randint(jax.random.fold_in(rng, axis), (), 0, dims[axis]) for axis in range(len(dims))]
    drawn = drawn.at[tuple(place)].set(smallest)
    longest = dims.index(max(dims))
    place[longest] = (place[longest] + 1) % dims[longest]
    return drawn.at[tuple(place)].set(high)


def level_of(own_key, shape, cuts, smallest, top_value):
    level = 1.0
    for dim, shards_of in cuts:
        steps = jax.random.uniform(jax.random.fold_in(jax.random.fold_in(own_key, 6), dim), (shards_of,), jnp.float32, smallest / len(cuts), top_value / len(cuts))
        level = level * jnp.repeat(jnp.exp(steps), shape[dim] // shards_of).reshape((-1,) + (1,) * (len(shape) - 1 - dim))
    return level


def bell_draw(key, dims, deviation, limit, pieces=(), held_as=jnp.bfloat16):
    drawn = deviation * jax.random.normal(key, dims, jnp.float32)
    if pieces:
        drawn = drawn * level_of(key, dims, pieces, -0.22, 0.18)
    return jnp.clip(drawn, -limit, limit).astype(held_as)


def setup_inputs(seed: int = 0) -> dict:
    arg_keys = jax.random.split(jax.random.key(seed), 6)
    samples = draw_samples(jax.random.fold_in(arg_keys[5], 71), 0)
    targets = draw_targets(jax.random.fold_in(arg_keys[5], 71), 0)
    row_slot = draw_row_slot(jax.random.fold_in(arg_keys[5], 71), 0)
    hot_group = place_ends(jax.random.randint(arg_keys[3], (N_DEV,), 0, N_GRP), jax.random.fold_in(arg_keys[3], 1), 0, N_GRP - 1).astype(jnp.int32)
    anchor = bell_draw(arg_keys[4], (LISTS, D, D), D ** -0.5, 0.21875, ((0, 512),))
    return dict(samples=samples, targets=targets, row_slot=row_slot, hot_group=hot_group, anchor=anchor)


first_coef = 3.4445
third_coef = -4.775
fifth_coef = 2.0315

def polar_factor(matrix):
    rounded = matrix.astype(jnp.bfloat16)
    gram_matrix = jnp.dot(rounded, rounded.T, preferred_element_type=jnp.float32)
    norm_value = jnp.sqrt(jnp.sum(gram_matrix * gram_matrix) + 1e-06)
    iterate = (matrix / jnp.sqrt(norm_value)).astype(jnp.bfloat16)
    square = (gram_matrix / norm_value).astype(jnp.bfloat16)
    update = iterate.astype(jnp.float32)
    for sweep in range(ITERS):
        if sweep > 0:
            square = jnp.dot(iterate, iterate.T, preferred_element_type=jnp.float32).astype(jnp.bfloat16)
        squared_twice = jnp.dot(square, square, preferred_element_type=jnp.float32)
        blend = (third_coef * square.astype(jnp.float32) + fifth_coef * squared_twice).astype(jnp.bfloat16)
        update = first_coef * iterate.astype(jnp.float32) + jnp.dot(blend, iterate, preferred_element_type=jnp.float32)
        if sweep + 1 < ITERS:
            iterate = update.astype(jnp.bfloat16)
    return (math.sqrt(D) * update).astype(jnp.bfloat16)

def group_order(values, target_rows, slots):
    labels = jnp.arange(2 * N_DEV, dtype=jnp.int32)
    order = jnp.argsort(slots, stable=True)
    padding = jnp.zeros((ROWS_DEV, D), jnp.bfloat16)
    sorted_values = jnp.concatenate([jnp.take(values, order, axis=0), padding], axis=0)
    sorted_targets = jnp.concatenate([jnp.take(target_rows, order, axis=0), padding], axis=0)
    counts = lax.optimization_barrier(jnp.sum((slots[:, None] == labels[None, :]).astype(jnp.int32), axis=0)).astype(jnp.int32)
    starts = (jnp.cumsum(counts) - counts).astype(jnp.int32)
    return (sorted_values, sorted_targets, starts, counts)

def bucket_sum(ordered, label):
    sorted_values, sorted_targets, starts, counts = ordered
    block_values = lax.dynamic_slice_in_dim(sorted_values, starts[label], ROWS_DEV, 0)
    block_targets = lax.dynamic_slice_in_dim(sorted_targets, starts[label], ROWS_DEV, 0)
    filled = jnp.arange(ROWS_DEV, dtype=jnp.int32) < counts[label]
    block_targets = jnp.where(filled[:, None], block_targets, jnp.zeros((), jnp.bfloat16))
    return jnp.dot(block_targets.T, block_values, preferred_element_type=jnp.float32)

def reference(samples, targets, row_slot, hot_group, anchor):
    per_group = N_DEV * ROWS_DEV
    values = samples.reshape(N_GRP, per_group, D)
    target_rows = targets.reshape(N_GRP, per_group, D)
    slots = row_slot.reshape(N_GRP, per_group)
    weight = math.sqrt(D * ROWS_DEV) / 2.0

    def hot_step(summed, group_rows):
        ordered = group_order(group_rows[0], group_rows[1], group_rows[2])

        def replica_sum(column):
            return bucket_sum(ordered, column + N_DEV)
        return (summed + lax.map(replica_sum, jnp.arange(N_DEV, dtype=jnp.int32)), None)
    hot_total, _ = lax.scan(hot_step, jnp.zeros((N_DEV, D, D), jnp.float32), (values, target_rows, slots))

    def cold_group(group_rows):
        group_values, group_targets, group_slots, group_index = group_rows
        ordered = group_order(group_values, group_targets, group_slots)

        def one_list(column):
            owned = hot_group[column] == group_index
            matrix = bucket_sum(ordered, column) + jnp.where(owned, hot_total[column], jnp.zeros((D, D), jnp.float32))
            matrix = matrix + weight * anchor[group_index * N_DEV + column].astype(jnp.float32)
            return polar_factor(matrix)
        return lax.map(one_list, jnp.arange(N_DEV, dtype=jnp.int32))
    rotations = lax.map(cold_group, (values, target_rows, slots, jnp.arange(N_GRP, dtype=jnp.int32)))
    return rotations.reshape(N_GRP * N_DEV, D, D)
```

```python
import functools
import math

import jax
import jax.numpy as jnp
from jax import lax
from jax.experimental import pallas as pl
from jax.experimental.pallas import tpu as pltpu
from jax.sharding import PartitionSpec as P

MESH = pl.DeviceIdType.MESH
ITERS = 2
first_coef = 3.4445
third_coef = -4.775
fifth_coef = 2.0315

NX, NY, NZ, NC = 4, 8, 8, 2
COLUMNS = 32
CAP = 16
D = 768
PIECE = D // NZ
HALF = PIECE // 2


def device_at(x, y, z, c):
    return (lax.rem(y, 2) * NZ + z, x * 8 + lax.div(y, 2) * 2 + c)


def exchange(
    slot_ref, samples_ref, targets_ref, hot_ref, cold_ref,
    send_hot, send_cold, recv_hot, recv_cold, hot_sum, rs_first, rs_own, rs_in, partial, moved,
    hot_ssem, hot_rsem, cold_ssem, cold_rsem, rs_ssem, rs_rsem, mv_ssem, mv_rsem, ag_ssem, ag_rsem,
):
    grp, dev = lax.axis_index("grp"), lax.axis_index("dev")
    y_lo, z = lax.div(grp, NZ), lax.rem(grp, NZ)
    x, y_hi, c = lax.div(dev, 8), lax.rem(lax.div(dev, 2), 4), lax.rem(dev, 2)
    y = 2 * y_hi + y_lo
    wrap_x = lambda v: lax.rem(v + NX, NX)
    wrap_y = lambda v: lax.rem(v + NY, NY)
    wrap_z = lambda v: lax.rem(v + NZ, NZ)

    def offsets(r):
        return lax.div(r, 8), lax.rem(lax.div(r, 2), 4), lax.rem(r, 2)

    def hot_step(q, core):
        return q - 4 * lax.div(2 * q + core, 5)

    def hot_target(r):
        dx, q, dc = offsets(r)
        core = lax.rem(c + dc, 2)
        row = wrap_y(y + hot_step(q, core))
        col = wrap_x(x + dx) * 8 + lax.rem(row, 4) * 2 + core
        return device_at(wrap_x(x + dx), row, z, core), col

    def hot_source(r):
        dx, q, dc = offsets(r)
        return device_at(wrap_x(x - dx), wrap_y(y - hot_step(q, c)), z, lax.rem(c + dc, 2))

    def cold_target(r):
        dx, q, dc = offsets(r)
        core, hi = lax.rem(c + dc, 2), lax.rem(y_hi + q, 4)
        col = wrap_x(x + dx) * 8 + hi * 2 + core
        return (grp, col), col

    def cold_source(r):
        dx, q, dc = offsets(r)
        return (grp, wrap_x(x - dx) * 8 + lax.rem(y_hi + 4 - q, 4) * 2 + lax.rem(c + dc, 2))

    z_ids = (device_at(x, y, wrap_z(z - 1), c), device_at(x, y, wrap_z(z + 1), c))
    move_rows = tuple(2 * lax.rem(y, 4) + t for t in range(2))
    from_rows = tuple(y_hi + 4 * s for s in range(2))

    barrier = pltpu.get_barrier_semaphore()

    def greet(r, carry):
        pl.semaphore_signal(barrier, inc=1, device_id=hot_source(r), device_id_type=MESH)
        pl.semaphore_signal(barrier, inc=1, device_id=cold_source(r), device_id_type=MESH)
        return carry

    lax.fori_loop(1, COLUMNS, greet, 0)
    for other in z_ids:
        pl.semaphore_signal(barrier, inc=1, device_id=other, device_id_type=MESH)
    for row in from_rows:
        @pl.when(row != y)
        def _():
            pl.semaphore_signal(barrier, inc=1, device_id=device_at(x, row, z, c), device_id_type=MESH)

    slot = slot_ref[...]
    rows = slot.shape[1]
    member = (lax.broadcasted_iota(jnp.int32, (2 * COLUMNS, rows), 0) == slot).astype(jnp.float32)
    before = (
        lax.broadcasted_iota(jnp.int32, (rows, rows), 0) < lax.broadcasted_iota(jnp.int32, (rows, rows), 1)
    ).astype(jnp.float32).astype(jnp.bfloat16)
    count = jnp.dot(member.astype(jnp.bfloat16), before, preferred_element_type=jnp.float32)
    rank = jnp.sum(count * member, axis=0, keepdims=True)
    place = slot * CAP + rank.astype(jnp.int32)

    def sort_into(out, base):
        pick = (
            (lax.broadcasted_iota(jnp.int32, (COLUMNS * CAP, rows), 0) + base) == place
        ).astype(jnp.float32).astype(jnp.bfloat16)
        for ref, lane in ((samples_ref, 0), (targets_ref, D)):
            picked = jnp.dot(pick, ref[...], preferred_element_type=jnp.float32).astype(jnp.bfloat16)
            out[:, :, lane:lane + D] = picked.reshape(COLUMNS, CAP, D)

    sort_into(send_hot, COLUMNS * CAP)

    elsewhere = 2 - lax.div(y + 1, NY) - lax.div(NY - y, NY)
    pl.semaphore_wait(barrier, 2 * (COLUMNS - 1) + 2 + elsewhere)

    def send_rows(target, out, into, ssem, rsem, first=1, last=COLUMNS):
        def body(r, carry):
            where, col = target(r)
            pltpu.make_async_remote_copy(
                src_ref=out.at[col], dst_ref=into.at[r], send_sem=ssem, recv_sem=rsem,
                device_id=where, device_id_type=MESH,
            ).start()
            return carry
        lax.fori_loop(first, last, body, 0)

    def wait_rows(ref, sem):
        many = ref.at[pl.ds(1, COLUMNS - 1)]
        pltpu.make_async_copy(many, many, sem).wait()

    def outer_sum(ref):
        both = ref[...].reshape(COLUMNS * CAP, 2 * D)
        return lax.dot_general(
            both[:, D:], both[:, :D], (((0,), (0,)), ((), ())), preferred_element_type=jnp.float32
        )

    send_rows(hot_target, send_hot, recv_hot, hot_ssem, hot_rsem)
    recv_hot[0] = send_hot[hot_target(0)[1]]
    sort_into(send_cold, 0)
    recv_cold[0] = send_cold[dev]
    wait_rows(send_hot, hot_ssem)
    started = [1]

    def drip(n):
        first, last = started[0], min(started[0] + n, COLUMNS)
        if first < last:
            send_rows(cold_target, send_cold, recv_cold, cold_ssem, cold_rsem, first, last)
        started[0] = last

    drip(3)
    wait_rows(recv_hot, hot_rsem)
    hot_sum[...] = outer_sum(recv_hot)

    def rows_of(piece, sub):
        return pl.ds(pl.multiple_of(piece * PIECE + sub * HALF, CAP), HALF)

    def rs_piece(way, k):
        return wrap_z(z + (k - 5 if way == 0 else 5 - k) + NZ)

    def rs_send(way, k, sub, src):
        copy = pltpu.make_async_remote_copy(
            src_ref=src, dst_ref=rs_in.at[way, k - 1, pl.ds(sub * HALF, HALF)],
            send_sem=rs_ssem.at[way, k - 1, sub], recv_sem=rs_rsem.at[way, k - 1, sub],
            device_id=z_ids[way], device_id_type=MESH,
        )
        copy.start()
        pending.append(copy)

    def rs_wait(way, k, sub):
        drip(1)
        part = rs_in.at[way, k - 1, pl.ds(sub * HALF, HALF)]
        pltpu.make_async_copy(part, part, rs_rsem.at[way, k - 1, sub]).wait()
        return part

    pending = []
    for way in range(2):
        rs_first[way] = hot_sum[rows_of(rs_piece(way, 1), way), :].astype(jnp.bfloat16)
        rs_send(way, 1, way, rs_first.at[way])
    for way in range(2):
        rs_own[way] = hot_sum[rows_of(rs_piece(way, 2), 1 - way), :].astype(jnp.bfloat16)
        rs_send(way, 2, 1 - way, rs_own.at[way])
    for k in range(2, 5):
        for turn in range(2):
            for way in range(2):
                sub = 1 - way if turn == 0 else way
                if k == 2 and turn == 0:
                    continue
                part = rs_wait(way, k - 1, sub)
                part[...] = (
                    part[...].astype(jnp.float32) + hot_sum[rows_of(rs_piece(way, k), sub), :]
                ).astype(jnp.bfloat16)
                rs_send(way, k, sub, part)

    for sub in range(2):
        total = hot_sum[rows_of(z, sub), :]
        for way in range(2):
            total = total + rs_wait(way, 4, sub)[...].astype(jnp.float32)
        half = pl.ds(sub * HALF, HALF)
        partial[half, :] = total.astype(jnp.bfloat16)
        for t, row in enumerate(move_rows):
            slot_no = lax.div(y, 4)

            @pl.when(row != y)
            def _():
                pltpu.make_async_remote_copy(
                    src_ref=partial.at[half], dst_ref=moved.at[slot_no, half],
                    send_sem=mv_ssem.at[t, sub], recv_sem=mv_rsem.at[slot_no, sub],
                    device_id=device_at(x, row, z, c), device_id_type=MESH,
                ).start()

            @pl.when(row == y)
            def _():
                pltpu.make_async_copy(
                    partial.at[half], moved.at[slot_no, half], mv_rsem.at[slot_no, sub]
                ).start()

    def ag_copy(way, k, sub, piece):
        part = hot_ref.at[rows_of(piece, sub)]
        return pltpu.make_async_remote_copy(
            src_ref=part, dst_ref=part, send_sem=ag_ssem.at[way, k - 1, sub],
            recv_sem=ag_rsem.at[way, k - 1, sub], device_id=z_ids[way], device_id_type=MESH,
        )

    def ag_send(way, k, sub):
        piece = wrap_z(z + (k - 1 if way == 0 else 1 - k))
        copy = ag_copy(way, k, sub, piece)
        copy.start()
        pending.append(copy)

    for sub in range(2):
        half = pl.ds(sub * HALF, HALF)
        total = jnp.zeros((HALF, D), jnp.float32)
        for s in range(2):
            part = moved.at[s, half]
            drip(1)
            pltpu.make_async_copy(part, part, mv_rsem.at[s, sub]).wait()
            total = total + part[...].astype(jnp.float32)
        hot_ref[rows_of(z, sub), :] = total.astype(jnp.bfloat16)
        for way in range(2):
            ag_send(way, 1, sub)
    for k in range(1, 5):
        for sub in range(2):
            for way in range(2):
                if k == 4 and sub != way:
                    continue
                drip(1)
                ag_copy(way, k, sub, wrap_z(z + (k if way == 0 else -k))).wait_recv()
                if k < 3 or (k == 3 and sub == way):
                    ag_send(way, k + 1, sub)

    drip(COLUMNS)
    wait_rows(recv_cold, cold_rsem)
    cold_ref[...] = outer_sum(recv_cold)

    wait_rows(send_cold, cold_ssem)
    for copy in pending:
        copy.wait_send()
    for sub in range(2):
        for t, row in enumerate(move_rows):
            @pl.when(row != y)
            def _():
                part = partial.at[pl.ds(sub * HALF, HALF)]
                pltpu.make_async_copy(part, part, mv_ssem.at[t, sub]).wait()


def polar(weight, owned_ref, cold_ref, hot_ref, anchor_ref, out_ref):
    hot = hot_ref[...].astype(jnp.float32)
    matrix = cold_ref[...] + jnp.where(owned_ref[0] > 0, hot, jnp.zeros_like(hot))
    matrix = matrix + weight * anchor_ref[...].astype(jnp.float32)
    rounded = matrix.astype(jnp.bfloat16)
    last = (((1,), (1,)), ((), ()))
    gram = lax.dot_general(rounded, rounded, last, preferred_element_type=jnp.float32)
    norm = jnp.sqrt(jnp.sum(gram * gram) + 1e-06)
    iterate = (matrix / jnp.sqrt(norm)).astype(jnp.bfloat16)
    square = (gram / norm).astype(jnp.bfloat16)
    update = None
    for sweep in range(ITERS):
        if sweep > 0:
            square = lax.dot_general(iterate, iterate, last, preferred_element_type=jnp.float32)
            square = square.astype(jnp.bfloat16)
        twice = jnp.dot(square, square, preferred_element_type=jnp.float32)
        blend = (third_coef * square.astype(jnp.float32) + fifth_coef * twice).astype(jnp.bfloat16)
        update = first_coef * iterate.astype(jnp.float32) + jnp.dot(
            blend, iterate, preferred_element_type=jnp.float32
        )
        iterate = update.astype(jnp.bfloat16)
    out_ref[...] = (math.sqrt(D) * update).astype(jnp.bfloat16)


def shards(samples, targets, row_slot, hot_group, anchor):
    rows = samples.shape[0]
    vmem = pl.BlockSpec(memory_space=pltpu.VMEM)
    dma = pltpu.SemaphoreType.DMA
    hot, cold = pl.pallas_call(
        exchange,
        out_shape=(
            jax.ShapeDtypeStruct((D, D), jnp.bfloat16),
            jax.ShapeDtypeStruct((D, D), jnp.float32),
        ),
        in_specs=[vmem] * 3,
        out_specs=(vmem, vmem),
        scratch_shapes=[
            pltpu.VMEM((COLUMNS, CAP, 2 * D), jnp.bfloat16),
            pltpu.VMEM((COLUMNS, CAP, 2 * D), jnp.bfloat16),
            pltpu.VMEM((COLUMNS, CAP, 2 * D), jnp.bfloat16),
            pltpu.VMEM((COLUMNS, CAP, 2 * D), jnp.bfloat16),
            pltpu.VMEM((D, D), jnp.float32),
            pltpu.VMEM((2, HALF, D), jnp.bfloat16),
            pltpu.VMEM((2, HALF, D), jnp.bfloat16),
            pltpu.VMEM((2, 4, PIECE, D), jnp.bfloat16),
            pltpu.VMEM((PIECE, D), jnp.bfloat16),
            pltpu.VMEM((2, PIECE, D), jnp.bfloat16),
            dma, dma, dma, dma,
            dma((2, 4, 2)), dma((2, 4, 2)),
            dma((2, 2)), dma((2, 2)),
            dma((2, 4, 2)), dma((2, 4, 2)),
        ],
        compiler_params=pltpu.CompilerParams(
            collective_id=0, has_side_effects=True, vmem_limit_bytes=48 << 20
        ),
    )(row_slot.reshape(1, rows), samples, targets)
    owned = (lax.axis_index("grp") == hot_group).astype(jnp.int32)
    weight = math.sqrt(D * rows) / 2.0
    rotation = pl.pallas_call(
        functools.partial(polar, weight),
        out_shape=jax.ShapeDtypeStruct((D, D), jnp.bfloat16),
        in_specs=[pl.BlockSpec(memory_space=pltpu.SMEM)] + [vmem] * 3,
        out_specs=vmem,
        compiler_params=pltpu.CompilerParams(vmem_limit_bytes=48 << 20),
    )(owned, cold, hot, anchor[0])
    return rotation[None]


def solution(mesh):
    return jax.shard_map(
        shards,
        mesh=mesh,
        in_specs=(
            P(("grp", "dev"), None),
            P(("grp", "dev"), None),
            P(("grp", "dev")),
            P("dev"),
            P(("grp", "dev"), None, None),
        ),
        out_specs=P(("grp", "dev"), None, None),
        check_vma=False,
    )
```

```python
import functools
import math

import jax
import jax.numpy as jnp
from jax import lax
from jax.experimental import pallas as pl
from jax.experimental.pallas import tpu as pltpu
from jax.sharding import PartitionSpec as P

MESH = pl.DeviceIdType.MESH
ITERS = 2
first_coef = 3.4445
third_coef = -4.775
fifth_coef = 2.0315

NX, NY, NZ, NC = 4, 8, 8, 2
COLUMNS = 32
CAP = 16
D = 768
PIECE = D // NZ
SUBS = 2
SUB = PIECE // SUBS
FIRST, SECOND, PACE = 0, 3, 1


def device_at(x, y, z, c):
    return (lax.rem(y, 2) * NZ + z, x * 8 + lax.div(y, 2) * 2 + c)


def exchange(
    weight, slot_hbm, samples_hbm, targets_hbm, anchor_hbm, hot_ref, base_ref,
    slot_ref, samples_ref, targets_ref, anchor_ref,
    send_hot, send_cold, recv_hot, recv_cold, hot_sum, rs_first, rs_own, rs_in, partial, moved,
    in_sems, hot_ssem, hot_rsem, cold_ssem, cold_rsem, rs_ssem, rs_rsem, mv_ssem, mv_rsem, ag_ssem, ag_rsem,
):
    grp, dev = lax.axis_index("grp"), lax.axis_index("dev")
    y_lo, z = lax.div(grp, NZ), lax.rem(grp, NZ)
    x, y_hi, c = lax.div(dev, 8), lax.rem(lax.div(dev, 2), 4), lax.rem(dev, 2)
    y = 2 * y_hi + y_lo
    loads = [
        pltpu.make_async_copy(src, dst, in_sems.at[i])
        for i, (src, dst) in enumerate(
            ((slot_hbm, slot_ref), (samples_hbm, samples_ref), (targets_hbm, targets_ref), (anchor_hbm, anchor_ref))
        )
    ]
    for load in loads:
        load.start()
    wrap_x = lambda v: lax.rem(v + NX, NX)
    wrap_y = lambda v: lax.rem(v + NY, NY)
    wrap_z = lambda v: lax.rem(v + NZ, NZ)

    def offsets(r):
        return lax.div(r, 8), lax.rem(lax.div(r, 2), 4), lax.rem(r, 2)

    def hot_step(q, core):
        return q - 4 * lax.div(2 * q + core, 5)

    def hot_target(r):
        dx, q, dc = offsets(r)
        core = lax.rem(c + dc, 2)
        row = wrap_y(y + hot_step(q, core))
        col = wrap_x(x + dx) * 8 + lax.rem(row, 4) * 2 + core
        return device_at(wrap_x(x + dx), row, z, core), col

    def hot_source(r):
        dx, q, dc = offsets(r)
        return device_at(wrap_x(x - dx), wrap_y(y - hot_step(q, c)), z, lax.rem(c + dc, 2))

    def cold_target(r):
        dx, q, dc = offsets(r)
        core, hi = lax.rem(c + dc, 2), lax.rem(y_hi + q, 4)
        col = wrap_x(x + dx) * 8 + hi * 2 + core
        return (grp, col), col

    def cold_source(r):
        dx, q, dc = offsets(r)
        return (grp, wrap_x(x - dx) * 8 + lax.rem(y_hi + 4 - q, 4) * 2 + lax.rem(c + dc, 2))

    z_ids = (device_at(x, y, wrap_z(z - 1), c), device_at(x, y, wrap_z(z + 1), c))
    move_rows = tuple(2 * lax.rem(y, 4) + t for t in range(2))
    from_rows = tuple(y_hi + 4 * s for s in range(2))

    barrier = pltpu.get_barrier_semaphore()

    def greet(r, carry):
        pl.semaphore_signal(barrier, inc=1, device_id=hot_source(r), device_id_type=MESH)
        pl.semaphore_signal(barrier, inc=1, device_id=cold_source(r), device_id_type=MESH)
        return carry

    lax.fori_loop(1, COLUMNS, greet, 0)
    for other in z_ids:
        pl.semaphore_signal(barrier, inc=1, device_id=other, device_id_type=MESH)
    for row in from_rows:
        @pl.when(row != y)
        def _():
            pl.semaphore_signal(barrier, inc=1, device_id=device_at(x, row, z, c), device_id_type=MESH)

    loads[0].wait()
    slot = slot_ref[...]
    rows = slot.shape[1]
    member = (lax.broadcasted_iota(jnp.int32, (2 * COLUMNS, rows), 0) == slot).astype(jnp.float32)
    before = (
        lax.broadcasted_iota(jnp.int32, (rows, rows), 0) < lax.broadcasted_iota(jnp.int32, (rows, rows), 1)
    ).astype(jnp.float32).astype(jnp.bfloat16)
    count = jnp.dot(member.astype(jnp.bfloat16), before, preferred_element_type=jnp.float32)
    rank = jnp.sum(count * member, axis=0, keepdims=True)
    place = slot * CAP + rank.astype(jnp.int32)

    def sort_into(out, base):
        pick = (
            (lax.broadcasted_iota(jnp.int32, (COLUMNS * CAP, rows), 0) + base) == place
        ).astype(jnp.float32).astype(jnp.bfloat16)
        for ref, lane in ((samples_ref, 0), (targets_ref, D)):
            picked = jnp.dot(pick, ref[...], preferred_element_type=jnp.float32).astype(jnp.bfloat16)
            out[:, :, lane:lane + D] = picked.reshape(COLUMNS, CAP, D)

    loads[1].wait()
    loads[2].wait()
    sort_into(send_hot, COLUMNS * CAP)

    elsewhere = 2 - lax.div(y + 1, NY) - lax.div(NY - y, NY)
    pl.semaphore_wait(barrier, 2 * (COLUMNS - 1) + 2 + elsewhere)

    def send_rows(target, out, into, ssem, rsem, first=1, last=COLUMNS):
        def body(r, carry):
            where, col = target(r)
            pltpu.make_async_remote_copy(
                src_ref=out.at[col], dst_ref=into.at[r], send_sem=ssem, recv_sem=rsem,
                device_id=where, device_id_type=MESH,
            ).start()
            return carry
        lax.fori_loop(first, last, body, 0)

    def wait_rows(ref, sem):
        many = ref.at[pl.ds(1, COLUMNS - 1)]
        pltpu.make_async_copy(many, many, sem).wait()

    def outer_sum(ref):
        both = ref[...].reshape(COLUMNS * CAP, 2 * D)
        return lax.dot_general(
            both[:, D:], both[:, :D], (((0,), (0,)), ((), ())), preferred_element_type=jnp.float32
        )

    started = [1]
    events = [0]

    def start_cold(n):
        first, last = started[0], min(started[0] + n, COLUMNS)
        if first < last:
            send_rows(cold_target, send_cold, recv_cold, cold_ssem, cold_rsem, first, last)
        started[0] = last

    def pace():
        events[0] += 1
        if events[0] % PACE == 0:
            start_cold(1)

    send_rows(hot_target, send_hot, recv_hot, hot_ssem, hot_rsem)
    recv_hot[0] = send_hot[hot_target(0)[1]]
    sort_into(send_cold, 0)
    recv_cold[0] = send_cold[dev]
    start_cold(FIRST)
    wait_rows(send_hot, hot_ssem)
    start_cold(SECOND)
    wait_rows(recv_hot, hot_rsem)
    hot_sum[...] = outer_sum(recv_hot)

    def rows_of(piece, sub, subs=1):
        return pl.ds(pl.multiple_of(piece * PIECE + sub * SUB, CAP), subs * SUB)

    far = (range(SUBS // 2), range(SUBS // 2, SUBS))
    order = (tuple(far[1]) + tuple(far[0]), tuple(far[0]) + tuple(far[1]))

    def rs_piece(way, k):
        return wrap_z(z + (k - 5 if way == 0 else 5 - k) + NZ)

    def rs_slot(way, k, sub):
        return rs_in.at[way, k - 1, pl.ds(sub * SUB, SUB)]

    def rs_send(way, k, sub, src):
        copy = pltpu.make_async_remote_copy(
            src_ref=src, dst_ref=rs_slot(way, k, sub),
            send_sem=rs_ssem.at[way, k - 1, sub], recv_sem=rs_rsem.at[way, k - 1, sub],
            device_id=z_ids[way], device_id_type=MESH,
        )
        copy.start()
        pending.append(copy)

    def rs_wait(way, k, sub):
        pace()
        part = rs_slot(way, k, sub)
        pltpu.make_async_copy(part, part, rs_rsem.at[way, k - 1, sub]).wait()
        return part

    pending = []
    for k, kept in ((1, rs_first), (2, rs_own)):
        for way in range(2):
            subs = far[way] if k == 1 else far[1 - way]
            kept[way] = hot_sum[rows_of(rs_piece(way, k), subs[0], SUBS // 2), :].astype(jnp.bfloat16)
        for i in range(SUBS // 2):
            for way in range(2):
                subs = far[way] if k == 1 else far[1 - way]
                rs_send(way, k, subs[i], kept.at[way, pl.ds(i * SUB, SUB)])
    for k in range(2, 5):
        for turn in range(SUBS):
            for way in range(2):
                sub = order[way][turn]
                if k == 2 and sub not in far[way]:
                    continue
                part = rs_wait(way, k - 1, sub)
                part[...] = (
                    part[...].astype(jnp.float32) + hot_sum[rows_of(rs_piece(way, k), sub), :]
                ).astype(jnp.bfloat16)
                rs_send(way, k, sub, part)

    slot_no = lax.div(y, 4)
    for sub in range(SUBS):
        total = hot_sum[rows_of(z, sub), :]
        for way in range(2):
            total = total + rs_wait(way, 4, sub)[...].astype(jnp.float32)
        part = pl.ds(sub * SUB, SUB)
        partial[part, :] = total.astype(jnp.bfloat16)
        for t, row in enumerate(move_rows):
            @pl.when(row != y)
            def _():
                pltpu.make_async_remote_copy(
                    src_ref=partial.at[part], dst_ref=moved.at[slot_no, part],
                    send_sem=mv_ssem.at[t, sub], recv_sem=mv_rsem.at[slot_no, sub],
                    device_id=device_at(x, row, z, c), device_id_type=MESH,
                ).start()

            @pl.when(row == y)
            def _():
                pltpu.make_async_copy(
                    partial.at[part], moved.at[slot_no, part], mv_rsem.at[slot_no, sub]
                ).start()

    def ag_copy(way, k, sub, piece):
        part = hot_ref.at[rows_of(piece, sub)]
        return pltpu.make_async_remote_copy(
            src_ref=part, dst_ref=part, send_sem=ag_ssem.at[way, k - 1, sub],
            recv_sem=ag_rsem.at[way, k - 1, sub], device_id=z_ids[way], device_id_type=MESH,
        )

    def ag_send(way, k, sub):
        copy = ag_copy(way, k, sub, wrap_z(z + (k - 1 if way == 0 else 1 - k)))
        copy.start()
        pending.append(copy)

    for sub in range(SUBS):
        part = pl.ds(sub * SUB, SUB)
        total = jnp.zeros((SUB, D), jnp.float32)
        for s in range(2):
            pace()
            come = moved.at[s, part]
            pltpu.make_async_copy(come, come, mv_rsem.at[s, sub]).wait()
            total = total + come[...].astype(jnp.float32)
        hot_ref[rows_of(z, sub), :] = total.astype(jnp.bfloat16)
        for way in range(2):
            ag_send(way, 1, sub)
    for k in range(1, 5):
        for sub in range(SUBS):
            for way in range(2):
                if k == 4 and sub not in far[way]:
                    continue
                pace()
                ag_copy(way, k, sub, wrap_z(z + (k if way == 0 else -k))).wait_recv()
                if k < 3 or (k == 3 and sub in far[way]):
                    ag_send(way, k + 1, sub)

    start_cold(COLUMNS)
    loads[3].wait()
    wait_rows(recv_cold, cold_rsem)
    base_ref[...] = outer_sum(recv_cold) + weight * anchor_ref[...].astype(jnp.float32)

    wait_rows(send_cold, cold_ssem)
    for copy in pending:
        copy.wait_send()
    for sub in range(SUBS):
        for t, row in enumerate(move_rows):
            @pl.when(row != y)
            def _():
                part = partial.at[pl.ds(sub * SUB, SUB)]
                pltpu.make_async_copy(part, part, mv_ssem.at[t, sub]).wait()


def polar(owned_ref, base_ref, hot_ref, out_ref):
    hot = hot_ref[...].astype(jnp.float32)
    matrix = base_ref[...] + jnp.where(owned_ref[0] > 0, hot, jnp.zeros_like(hot))
    rounded = matrix.astype(jnp.bfloat16)
    last = (((1,), (1,)), ((), ()))
    gram = lax.dot_general(rounded, rounded, last, preferred_element_type=jnp.float32)
    norm = jnp.sqrt(jnp.sum(gram * gram) + 1e-06)
    iterate = (matrix * (1.0 / jnp.sqrt(norm))).astype(jnp.bfloat16)
    square = (gram * (1.0 / norm)).astype(jnp.bfloat16)
    update = None
    for sweep in range(ITERS):
        if sweep > 0:
            square = lax.dot_general(iterate, iterate, last, preferred_element_type=jnp.float32)
            square = square.astype(jnp.bfloat16)
        twice = jnp.dot(square, square, preferred_element_type=jnp.float32)
        blend = (third_coef * square.astype(jnp.float32) + fifth_coef * twice).astype(jnp.bfloat16)
        update = first_coef * iterate.astype(jnp.float32) + jnp.dot(
            blend, iterate, preferred_element_type=jnp.float32
        )
        iterate = update.astype(jnp.bfloat16)
    out_ref[...] = (math.sqrt(D) * update).astype(jnp.bfloat16)


def shards(samples, targets, row_slot, hot_group, anchor):
    rows = samples.shape[0]
    vmem = pl.BlockSpec(memory_space=pltpu.VMEM)
    dma = pltpu.SemaphoreType.DMA
    hbm = pl.BlockSpec(memory_space=pltpu.HBM)
    weight = math.sqrt(D * rows) / 2.0
    hot, base = pl.pallas_call(
        functools.partial(exchange, weight),
        out_shape=(
            jax.ShapeDtypeStruct((D, D), jnp.bfloat16),
            jax.ShapeDtypeStruct((D, D), jnp.float32),
        ),
        in_specs=[hbm] * 4,
        out_specs=(vmem, vmem),
        scratch_shapes=[
            pltpu.VMEM((1, rows), jnp.int32),
            pltpu.VMEM((rows, D), jnp.bfloat16),
            pltpu.VMEM((rows, D), jnp.bfloat16),
            pltpu.VMEM((D, D), jnp.bfloat16),
            pltpu.VMEM((COLUMNS, CAP, 2 * D), jnp.bfloat16),
            pltpu.VMEM((COLUMNS, CAP, 2 * D), jnp.bfloat16),
            pltpu.VMEM((COLUMNS, CAP, 2 * D), jnp.bfloat16),
            pltpu.VMEM((COLUMNS, CAP, 2 * D), jnp.bfloat16),
            pltpu.VMEM((D, D), jnp.float32),
            pltpu.VMEM((2, PIECE // 2, D), jnp.bfloat16),
            pltpu.VMEM((2, PIECE // 2, D), jnp.bfloat16),
            pltpu.VMEM((2, 4, PIECE, D), jnp.bfloat16),
            pltpu.VMEM((PIECE, D), jnp.bfloat16),
            pltpu.VMEM((2, PIECE, D), jnp.bfloat16),
            dma((4,)), dma, dma, dma, dma,
            dma((2, 4, SUBS)), dma((2, 4, SUBS)),
            dma((2, SUBS)), dma((2, SUBS)),
            dma((2, 4, SUBS)), dma((2, 4, SUBS)),
        ],
        compiler_params=pltpu.CompilerParams(
            collective_id=0, has_side_effects=True, vmem_limit_bytes=24 << 20
        ),
    )(*(
        pltpu.with_memory_space_constraint(a, pltpu.HBM)
        for a in (row_slot.reshape(1, rows), samples, targets, anchor[0])
    ))
    owned = (lax.axis_index("grp") == hot_group).astype(jnp.int32)
    rotation = pl.pallas_call(
        polar,
        out_shape=jax.ShapeDtypeStruct((D, D), jnp.bfloat16),
        in_specs=[pl.BlockSpec(memory_space=pltpu.SMEM), vmem, vmem],
        out_specs=vmem,
        compiler_params=pltpu.CompilerParams(vmem_limit_bytes=24 << 20),
    )(owned, base, hot)
    return rotation[None]


def solution(mesh):
    return jax.shard_map(
        shards,
        mesh=mesh,
        in_specs=(
            P(("grp", "dev"), None),
            P(("grp", "dev"), None),
            P(("grp", "dev")),
            P("dev"),
            P(("grp", "dev"), None, None),
        ),
        out_specs=P(("grp", "dev"), None, None),
        check_vma=False,
    )
```

```python
import functools
import math

import jax
import jax.numpy as jnp
from jax import lax
from jax.experimental import pallas as pl
from jax.experimental.pallas import tpu as pltpu
from jax.sharding import PartitionSpec as P

MESH = pl.DeviceIdType.MESH
ITERS = 2
first_coef = 3.4445
third_coef = -4.775
fifth_coef = 2.0315

NX, NY, NZ, NC = 4, 8, 8, 2
COLUMNS = 32
CAP = 16
D = 768
PIECE = D // NZ
SUBS = 2
SUB = PIECE // SUBS
FIRST, SECOND, PACE = 0, 6, 1


def device_at(x, y, z, c):
    return (lax.rem(y, 2) * NZ + z, x * 8 + lax.div(y, 2) * 2 + c)


def exchange(
    weight, slot_hbm, samples_hbm, targets_hbm, anchor_hbm, hot_ref, base_ref,
    slot_ref, samples_ref, targets_ref, anchor_ref,
    send_hot, send_cold, recv_hot, recv_cold, hot_sum, rs_first, rs_own, rs_in, partial, moved,
    in_sems, hot_ssem, hot_rsem, cold_ssem, cold_rsem, rs_ssem, rs_rsem, mv_ssem, mv_rsem, ag_ssem, ag_rsem,
):
    grp, dev = lax.axis_index("grp"), lax.axis_index("dev")
    y_lo, z = lax.div(grp, NZ), lax.rem(grp, NZ)
    x, y_hi, c = lax.div(dev, 8), lax.rem(lax.div(dev, 2), 4), lax.rem(dev, 2)
    y = 2 * y_hi + y_lo
    loads = [
        pltpu.make_async_copy(src, dst, in_sems.at[i])
        for i, (src, dst) in enumerate(
            ((slot_hbm, slot_ref), (samples_hbm, samples_ref), (targets_hbm, targets_ref), (anchor_hbm, anchor_ref))
        )
    ]
    for load in loads:
        load.start()
    wrap_x = lambda v: lax.rem(v + NX, NX)
    wrap_y = lambda v: lax.rem(v + NY, NY)
    wrap_z = lambda v: lax.rem(v + NZ, NZ)

    def offsets(r):
        return lax.div(r, 8), lax.rem(lax.div(r, 2), 4), lax.rem(r, 2)

    def gray(v):
        return v + lax.div(v, 2) * (1 - 2 * lax.rem(v, 2))

    def ordered(i):
        u, v = lax.rem(lax.div(i, 4), 4), lax.rem(i, 4)
        return 8 * gray(lax.rem(u + v, 4)) + 2 * gray(v) + lax.div(i, 16)

    def hot_step(q, core):
        return q - 4 * lax.div(2 * q + core, 5)

    def hot_target(r):
        dx, q, dc = offsets(r)
        core = lax.rem(c + dc, 2)
        row = wrap_y(y + hot_step(q, core))
        col = wrap_x(x + dx) * 8 + lax.rem(row, 4) * 2 + core
        return device_at(wrap_x(x + dx), row, z, core), col

    def hot_source(r):
        dx, q, dc = offsets(r)
        return device_at(wrap_x(x - dx), wrap_y(y - hot_step(q, c)), z, lax.rem(c + dc, 2))

    def cold_target(r):
        dx, q, dc = offsets(r)
        core, hi = lax.rem(c + dc, 2), lax.rem(y_hi + q, 4)
        col = wrap_x(x + dx) * 8 + hi * 2 + core
        return (grp, col), col

    def cold_source(r):
        dx, q, dc = offsets(r)
        return (grp, wrap_x(x - dx) * 8 + lax.rem(y_hi + 4 - q, 4) * 2 + lax.rem(c + dc, 2))

    z_ids = (device_at(x, y, wrap_z(z - 1), c), device_at(x, y, wrap_z(z + 1), c))
    move_rows = tuple(2 * lax.rem(y, 4) + t for t in range(2))
    from_rows = tuple(y_hi + 4 * s for s in range(2))

    barrier = pltpu.get_barrier_semaphore()

    def greet(r, carry):
        pl.semaphore_signal(barrier, inc=1, device_id=hot_source(r), device_id_type=MESH)
        pl.semaphore_signal(barrier, inc=1, device_id=cold_source(r), device_id_type=MESH)
        return carry

    lax.fori_loop(1, COLUMNS, greet, 0)
    for other in z_ids:
        pl.semaphore_signal(barrier, inc=1, device_id=other, device_id_type=MESH)
    for row in from_rows:
        @pl.when(row != y)
        def _():
            pl.semaphore_signal(barrier, inc=1, device_id=device_at(x, row, z, c), device_id_type=MESH)

    loads[0].wait()
    slot = slot_ref[...]
    rows = slot.shape[1]
    member = (lax.broadcasted_iota(jnp.int32, (2 * COLUMNS, rows), 0) == slot).astype(jnp.float32)
    before = (
        lax.broadcasted_iota(jnp.int32, (rows, rows), 0) < lax.broadcasted_iota(jnp.int32, (rows, rows), 1)
    ).astype(jnp.float32).astype(jnp.bfloat16)
    count = jnp.dot(member.astype(jnp.bfloat16), before, preferred_element_type=jnp.float32)
    rank = jnp.sum(count * member, axis=0, keepdims=True)
    place = slot * CAP + rank.astype(jnp.int32)

    def sort_into(out, base):
        pick = (
            (lax.broadcasted_iota(jnp.int32, (COLUMNS * CAP, rows), 0) + base) == place
        ).astype(jnp.float32).astype(jnp.bfloat16)
        for ref, lane in ((samples_ref, 0), (targets_ref, D)):
            picked = jnp.dot(pick, ref[...], preferred_element_type=jnp.float32).astype(jnp.bfloat16)
            out[:, :, lane:lane + D] = picked.reshape(COLUMNS, CAP, D)

    loads[1].wait()
    loads[2].wait()
    sort_into(send_hot, COLUMNS * CAP)

    elsewhere = 2 - lax.div(y + 1, NY) - lax.div(NY - y, NY)
    pl.semaphore_wait(barrier, 2 * (COLUMNS - 1) + 2 + elsewhere)

    def send_rows(target, out, into, ssem, rsem, first=1, last=COLUMNS):
        def body(i, carry):
            r = ordered(i)
            where, col = target(r)
            pltpu.make_async_remote_copy(
                src_ref=out.at[col], dst_ref=into.at[r], send_sem=ssem, recv_sem=rsem,
                device_id=where, device_id_type=MESH,
            ).start()
            return carry
        lax.fori_loop(first, last, body, 0)

    def wait_rows(ref, sem):
        many = ref.at[pl.ds(1, COLUMNS - 1)]
        pltpu.make_async_copy(many, many, sem).wait()

    def outer_sum(ref):
        both = ref[...].reshape(COLUMNS * CAP, 2 * D)
        return lax.dot_general(
            both[:, D:], both[:, :D], (((0,), (0,)), ((), ())), preferred_element_type=jnp.float32
        )

    started = [1]
    events = [0]

    def start_cold(n):
        first, last = started[0], min(started[0] + n, COLUMNS)
        if first < last:
            send_rows(cold_target, send_cold, recv_cold, cold_ssem, cold_rsem, first, last)
        started[0] = last

    def pace():
        events[0] += 1
        if events[0] % PACE == 0:
            start_cold(1)

    send_rows(hot_target, send_hot, recv_hot, hot_ssem, hot_rsem)
    recv_hot[0] = send_hot[hot_target(0)[1]]
    sort_into(send_cold, 0)
    recv_cold[0] = send_cold[dev]
    start_cold(FIRST)
    wait_rows(send_hot, hot_ssem)
    start_cold(SECOND)
    wait_rows(recv_hot, hot_rsem)
    hot_sum[...] = outer_sum(recv_hot)

    def rows_of(piece, sub, subs=1):
        return pl.ds(pl.multiple_of(piece * PIECE + sub * SUB, CAP), subs * SUB)

    far = (range(SUBS // 2), range(SUBS // 2, SUBS))
    order = (tuple(far[1]) + tuple(far[0]), tuple(far[0]) + tuple(far[1]))

    def rs_piece(way, k):
        return wrap_z(z + (k - 5 if way == 0 else 5 - k) + NZ)

    def rs_slot(way, k, sub):
        return rs_in.at[way, k - 1, pl.ds(sub * SUB, SUB)]

    def rs_send(way, k, sub, src):
        copy = pltpu.make_async_remote_copy(
            src_ref=src, dst_ref=rs_slot(way, k, sub),
            send_sem=rs_ssem.at[way, k - 1, sub], recv_sem=rs_rsem.at[way, k - 1, sub],
            device_id=z_ids[way], device_id_type=MESH,
        )
        copy.start()
        pending.append(copy)

    def rs_wait(way, k, sub):
        pace()
        part = rs_slot(way, k, sub)
        pltpu.make_async_copy(part, part, rs_rsem.at[way, k - 1, sub]).wait()
        return part

    pending = []
    for k, kept in ((1, rs_first), (2, rs_own)):
        for way in range(2):
            subs = far[way] if k == 1 else far[1 - way]
            kept[way] = hot_sum[rows_of(rs_piece(way, k), subs[0], SUBS // 2), :].astype(jnp.bfloat16)
        for i in range(SUBS // 2):
            for way in range(2):
                subs = far[way] if k == 1 else far[1 - way]
                rs_send(way, k, subs[i], kept.at[way, pl.ds(i * SUB, SUB)])
    for k in range(2, 5):
        for turn in range(SUBS):
            for way in range(2):
                sub = order[way][turn]
                if k == 2 and sub not in far[way]:
                    continue
                part = rs_wait(way, k - 1, sub)
                part[...] = (
                    part[...].astype(jnp.float32) + hot_sum[rows_of(rs_piece(way, k), sub), :]
                ).astype(jnp.bfloat16)
                rs_send(way, k, sub, part)

    slot_no = lax.div(y, 4)
    for sub in range(SUBS):
        total = hot_sum[rows_of(z, sub), :]
        for way in range(2):
            total = total + rs_wait(way, 4, sub)[...].astype(jnp.float32)
        part = pl.ds(sub * SUB, SUB)
        partial[part, :] = total.astype(jnp.bfloat16)
        for t, row in enumerate(move_rows):
            @pl.when(row != y)
            def _():
                pltpu.make_async_remote_copy(
                    src_ref=partial.at[part], dst_ref=moved.at[slot_no, part],
                    send_sem=mv_ssem.at[t, sub], recv_sem=mv_rsem.at[slot_no, sub],
                    device_id=device_at(x, row, z, c), device_id_type=MESH,
                ).start()

            @pl.when(row == y)
            def _():
                pltpu.make_async_copy(
                    partial.at[part], moved.at[slot_no, part], mv_rsem.at[slot_no, sub]
                ).start()

    def ag_copy(way, k, sub, piece):
        part = hot_ref.at[rows_of(piece, sub)]
        return pltpu.make_async_remote_copy(
            src_ref=part, dst_ref=part, send_sem=ag_ssem.at[way, k - 1, sub],
            recv_sem=ag_rsem.at[way, k - 1, sub], device_id=z_ids[way], device_id_type=MESH,
        )

    def ag_send(way, k, sub):
        copy = ag_copy(way, k, sub, wrap_z(z + (k - 1 if way == 0 else 1 - k)))
        copy.start()
        pending.append(copy)

    for sub in range(SUBS):
        part = pl.ds(sub * SUB, SUB)
        total = jnp.zeros((SUB, D), jnp.float32)
        for s in range(2):
            pace()
            come = moved.at[s, part]
            pltpu.make_async_copy(come, come, mv_rsem.at[s, sub]).wait()
            total = total + come[...].astype(jnp.float32)
        hot_ref[rows_of(z, sub), :] = total.astype(jnp.bfloat16)
        for way in range(2):
            ag_send(way, 1, sub)
    for k in range(1, 5):
        if k == 4:
            start_cold(COLUMNS)
            loads[3].wait()
            wait_rows(recv_cold, cold_rsem)
            base_ref[...] = outer_sum(recv_cold) + weight * anchor_ref[...].astype(jnp.float32)
        for sub in range(SUBS):
            for way in range(2):
                if k == 4 and sub not in far[way]:
                    continue
                pace()
                ag_copy(way, k, sub, wrap_z(z + (k if way == 0 else -k))).wait_recv()
                if k < 3 or (k == 3 and sub in far[way]):
                    ag_send(way, k + 1, sub)

    wait_rows(send_cold, cold_ssem)
    for copy in pending:
        copy.wait_send()
    for sub in range(SUBS):
        for t, row in enumerate(move_rows):
            @pl.when(row != y)
            def _():
                part = partial.at[pl.ds(sub * SUB, SUB)]
                pltpu.make_async_copy(part, part, mv_ssem.at[t, sub]).wait()


def polar(owned_ref, base_ref, hot_ref, out_ref):
    hot = hot_ref[...].astype(jnp.float32)
    matrix = base_ref[...] + jnp.where(owned_ref[0] > 0, hot, jnp.zeros_like(hot))
    rounded = matrix.astype(jnp.bfloat16)
    last = (((1,), (1,)), ((), ()))
    gram = lax.dot_general(rounded, rounded, last, preferred_element_type=jnp.float32)
    norm = jnp.sqrt(jnp.sum(gram * gram) + 1e-06)
    iterate = (matrix * (1.0 / jnp.sqrt(norm))).astype(jnp.bfloat16)
    square = (gram * (1.0 / norm)).astype(jnp.bfloat16)
    update = None
    for sweep in range(ITERS):
        if sweep > 0:
            square = lax.dot_general(iterate, iterate, last, preferred_element_type=jnp.float32)
            square = square.astype(jnp.bfloat16)
        twice = jnp.dot(square, square, preferred_element_type=jnp.float32)
        blend = (third_coef * square.astype(jnp.float32) + fifth_coef * twice).astype(jnp.bfloat16)
        update = first_coef * iterate.astype(jnp.float32) + jnp.dot(
            blend, iterate, preferred_element_type=jnp.float32
        )
        iterate = update.astype(jnp.bfloat16)
    out_ref[...] = (math.sqrt(D) * update).astype(jnp.bfloat16)


def shards(samples, targets, row_slot, hot_group, anchor):
    rows = samples.shape[0]
    vmem = pl.BlockSpec(memory_space=pltpu.VMEM)
    dma = pltpu.SemaphoreType.DMA
    hbm = pl.BlockSpec(memory_space=pltpu.HBM)
    weight = math.sqrt(D * rows) / 2.0
    hot, base = pl.pallas_call(
        functools.partial(exchange, weight),
        out_shape=(
            jax.ShapeDtypeStruct((D, D), jnp.bfloat16),
            jax.ShapeDtypeStruct((D, D), jnp.float32),
        ),
        in_specs=[hbm] * 4,
        out_specs=(vmem, vmem),
        scratch_shapes=[
            pltpu.VMEM((1, rows), jnp.int32),
            pltpu.VMEM((rows, D), jnp.bfloat16),
            pltpu.VMEM((rows, D), jnp.bfloat16),
            pltpu.VMEM((D, D), jnp.bfloat16),
            pltpu.VMEM((COLUMNS, CAP, 2 * D), jnp.bfloat16),
            pltpu.VMEM((COLUMNS, CAP, 2 * D), jnp.bfloat16),
            pltpu.VMEM((COLUMNS, CAP, 2 * D), jnp.bfloat16),
            pltpu.VMEM((COLUMNS, CAP, 2 * D), jnp.bfloat16),
            pltpu.VMEM((D, D), jnp.float32),
            pltpu.VMEM((2, PIECE // 2, D), jnp.bfloat16),
            pltpu.VMEM((2, PIECE // 2, D), jnp.bfloat16),
            pltpu.VMEM((2, 4, PIECE, D), jnp.bfloat16),
            pltpu.VMEM((PIECE, D), jnp.bfloat16),
            pltpu.VMEM((2, PIECE, D), jnp.bfloat16),
            dma((4,)), dma, dma, dma, dma,
            dma((2, 4, SUBS)), dma((2, 4, SUBS)),
            dma((2, SUBS)), dma((2, SUBS)),
            dma((2, 4, SUBS)), dma((2, 4, SUBS)),
        ],
        compiler_params=pltpu.CompilerParams(
            collective_id=0, has_side_effects=True, vmem_limit_bytes=24 << 20
        ),
    )(*(
        pltpu.with_memory_space_constraint(a, pltpu.HBM)
        for a in (row_slot.reshape(1, rows), samples, targets, anchor[0])
    ))
    owned = (lax.axis_index("grp") == hot_group).astype(jnp.int32)
    rotation = pl.pallas_call(
        polar,
        out_shape=jax.ShapeDtypeStruct((D, D), jnp.bfloat16),
        in_specs=[pl.BlockSpec(memory_space=pltpu.SMEM), vmem, vmem],
        out_specs=vmem,
        compiler_params=pltpu.CompilerParams(vmem_limit_bytes=24 << 20),
    )(owned, base, hot)
    return rotation[None]


def solution(mesh):
    return jax.shard_map(
        shards,
        mesh=mesh,
        in_specs=(
            P(("grp", "dev"), None),
            P(("grp", "dev"), None),
            P(("grp", "dev")),
            P("dev"),
            P(("grp", "dev"), None, None),
        ),
        out_specs=P(("grp", "dev"), None, None),
        check_vma=False,
    )
```

```python
import functools
import math

import jax
import jax.numpy as jnp
from jax import lax
from jax.experimental import pallas as pl
from jax.experimental.pallas import tpu as pltpu
from jax.sharding import PartitionSpec as P

MESH = pl.DeviceIdType.MESH
ITERS = 2
ROWS = 256
first_coef = 3.4445
third_coef = -4.775
fifth_coef = 2.0315

NX, NY, NZ, NC = 4, 8, 8, 2
COLUMNS = 32
CAP = 16
D = 768
PIECE = D // NZ
SUBS = 2
SUB = PIECE // SUBS
FIRST, SECOND, PACE = 0, 6, 1


def device_at(x, y, z, c):
    return (lax.rem(y, 2) * NZ + z, x * 8 + lax.div(y, 2) * 2 + c)


def exchange(
    weight, slot_hbm, samples_hbm, targets_hbm, anchor_hbm, hot_ref, base_ref,
    slot_ref, samples_ref, targets_ref, anchor_ref,
    send_hot, send_cold, recv_hot, recv_cold, hot_sum, rs_first, rs_own, rs_in, partial, moved,
    in_sems, hot_ssem, hot_rsem, cold_ssem, cold_rsem, rs_ssem, rs_rsem, mv_ssem, mv_rsem, ag_ssem, ag_rsem,
):
    grp, dev = lax.axis_index("grp"), lax.axis_index("dev")
    y_lo, z = lax.div(grp, NZ), lax.rem(grp, NZ)
    x, y_hi, c = lax.div(dev, 8), lax.rem(lax.div(dev, 2), 4), lax.rem(dev, 2)
    y = 2 * y_hi + y_lo
    loads = [
        pltpu.make_async_copy(src, dst, in_sems.at[i])
        for i, (src, dst) in enumerate(
            ((slot_hbm, slot_ref), (samples_hbm, samples_ref), (targets_hbm, targets_ref), (anchor_hbm, anchor_ref))
        )
    ]
    for load in loads:
        load.start()
    wrap_x = lambda v: lax.rem(v + NX, NX)
    wrap_y = lambda v: lax.rem(v + NY, NY)
    wrap_z = lambda v: lax.rem(v + NZ, NZ)

    def offsets(r):
        return lax.div(r, 8), lax.rem(lax.div(r, 2), 4), lax.rem(r, 2)

    def gray(v):
        return v + lax.div(v, 2) * (1 - 2 * lax.rem(v, 2))

    def ordered(i):
        u, v = lax.rem(lax.div(i, 4), 4), lax.rem(i, 4)
        return 8 * gray(lax.rem(u + v, 4)) + 2 * gray(v) + lax.div(i, 16)

    def hot_step(q, core):
        return q - 4 * lax.div(2 * q + core, 5)

    def hot_target(r):
        dx, q, dc = offsets(r)
        core = lax.rem(c + dc, 2)
        row = wrap_y(y + hot_step(q, core))
        col = wrap_x(x + dx) * 8 + lax.rem(row, 4) * 2 + core
        return device_at(wrap_x(x + dx), row, z, core), col

    def hot_source(r):
        dx, q, dc = offsets(r)
        return device_at(wrap_x(x - dx), wrap_y(y - hot_step(q, c)), z, lax.rem(c + dc, 2))

    def cold_target(r):
        dx, q, dc = offsets(r)
        core, hi = lax.rem(c + dc, 2), lax.rem(y_hi + q, 4)
        col = wrap_x(x + dx) * 8 + hi * 2 + core
        return (grp, col), col

    def cold_source(r):
        dx, q, dc = offsets(r)
        return (grp, wrap_x(x - dx) * 8 + lax.rem(y_hi + 4 - q, 4) * 2 + lax.rem(c + dc, 2))

    z_ids = (device_at(x, y, wrap_z(z - 1), c), device_at(x, y, wrap_z(z + 1), c))
    move_rows = tuple(2 * lax.rem(y, 4) + t for t in range(2))
    from_rows = tuple(y_hi + 4 * s for s in range(2))

    barrier = pltpu.get_barrier_semaphore()

    def greet(r, carry):
        pl.semaphore_signal(barrier, inc=1, device_id=hot_source(r), device_id_type=MESH)
        pl.semaphore_signal(barrier, inc=1, device_id=cold_source(r), device_id_type=MESH)
        return carry

    lax.fori_loop(1, COLUMNS, greet, 0)
    for other in z_ids:
        pl.semaphore_signal(barrier, inc=1, device_id=other, device_id_type=MESH)
    for row in from_rows:
        @pl.when(row != y)
        def _():
            pl.semaphore_signal(barrier, inc=1, device_id=device_at(x, row, z, c), device_id_type=MESH)

    loads[0].wait()
    slot = slot_ref[...]
    rows = slot.shape[1]
    member = (lax.broadcasted_iota(jnp.int32, (2 * COLUMNS, rows), 0) == slot).astype(jnp.float32)
    before = (
        lax.broadcasted_iota(jnp.int32, (rows, rows), 0) < lax.broadcasted_iota(jnp.int32, (rows, rows), 1)
    ).astype(jnp.float32).astype(jnp.bfloat16)
    count = jnp.dot(member.astype(jnp.bfloat16), before, preferred_element_type=jnp.float32)
    rank = jnp.sum(count * member, axis=0, keepdims=True)
    place = slot * CAP + rank.astype(jnp.int32)

    def sort_into(out, base):
        pick = (
            (lax.broadcasted_iota(jnp.int32, (COLUMNS * CAP, rows), 0) + base) == place
        ).astype(jnp.float32).astype(jnp.bfloat16)
        for ref, lane in ((samples_ref, 0), (targets_ref, D)):
            picked = jnp.dot(pick, ref[...], preferred_element_type=jnp.float32).astype(jnp.bfloat16)
            out[:, :, lane:lane + D] = picked.reshape(COLUMNS, CAP, D)

    loads[1].wait()
    loads[2].wait()
    sort_into(send_hot, COLUMNS * CAP)

    elsewhere = 2 - lax.div(y + 1, NY) - lax.div(NY - y, NY)
    pl.semaphore_wait(barrier, 2 * (COLUMNS - 1) + 2 + elsewhere)

    def send_rows(target, out, into, ssem, rsem, first=1, last=COLUMNS):
        def body(i, carry):
            r = ordered(i)
            where, col = target(r)
            pltpu.make_async_remote_copy(
                src_ref=out.at[col], dst_ref=into.at[r], send_sem=ssem, recv_sem=rsem,
                device_id=where, device_id_type=MESH,
            ).start()
            return carry
        lax.fori_loop(first, last, body, 0)

    def wait_rows(ref, sem):
        many = ref.at[pl.ds(1, COLUMNS - 1)]
        pltpu.make_async_copy(many, many, sem).wait()

    def outer_sum(ref):
        both = ref[...].reshape(COLUMNS * CAP, 2 * D)
        return lax.dot_general(
            both[:, D:], both[:, :D], (((0,), (0,)), ((), ())), preferred_element_type=jnp.float32
        )

    started = [1]
    events = [0]

    def start_cold(n):
        first, last = started[0], min(started[0] + n, COLUMNS)
        if first < last:
            send_rows(cold_target, send_cold, recv_cold, cold_ssem, cold_rsem, first, last)
        started[0] = last

    def pace():
        events[0] += 1
        if events[0] % PACE == 0:
            start_cold(1)

    send_rows(hot_target, send_hot, recv_hot, hot_ssem, hot_rsem)
    recv_hot[0] = send_hot[hot_target(0)[1]]
    sort_into(send_cold, 0)
    recv_cold[0] = send_cold[dev]
    start_cold(FIRST)
    wait_rows(send_hot, hot_ssem)
    start_cold(SECOND)
    wait_rows(recv_hot, hot_rsem)
    hot_sum[...] = outer_sum(recv_hot)

    def rows_of(piece, sub, subs=1):
        return pl.ds(pl.multiple_of(piece * PIECE + sub * SUB, CAP), subs * SUB)

    far = (range(SUBS // 2), range(SUBS // 2, SUBS))
    order = (tuple(far[1]) + tuple(far[0]), tuple(far[0]) + tuple(far[1]))

    def rs_piece(way, k):
        return wrap_z(z + (k - 5 if way == 0 else 5 - k) + NZ)

    def rs_slot(way, k, sub):
        return rs_in.at[way, k - 1, pl.ds(sub * SUB, SUB)]

    def rs_send(way, k, sub, src):
        copy = pltpu.make_async_remote_copy(
            src_ref=src, dst_ref=rs_slot(way, k, sub),
            send_sem=rs_ssem.at[way, k - 1, sub], recv_sem=rs_rsem.at[way, k - 1, sub],
            device_id=z_ids[way], device_id_type=MESH,
        )
        copy.start()
        pending.append(copy)

    def rs_wait(way, k, sub):
        pace()
        part = rs_slot(way, k, sub)
        pltpu.make_async_copy(part, part, rs_rsem.at[way, k - 1, sub]).wait()
        return part

    pending = []
    for k, kept in ((1, rs_first), (2, rs_own)):
        for way in range(2):
            subs = far[way] if k == 1 else far[1 - way]
            kept[way] = hot_sum[rows_of(rs_piece(way, k), subs[0], SUBS // 2), :].astype(jnp.bfloat16)
        for i in range(SUBS // 2):
            for way in range(2):
                subs = far[way] if k == 1 else far[1 - way]
                rs_send(way, k, subs[i], kept.at[way, pl.ds(i * SUB, SUB)])
    for k in range(2, 5):
        for turn in range(SUBS):
            for way in range(2):
                sub = order[way][turn]
                if k == 2 and sub not in far[way]:
                    continue
                part = rs_wait(way, k - 1, sub)
                part[...] = (
                    part[...].astype(jnp.float32) + hot_sum[rows_of(rs_piece(way, k), sub), :]
                ).astype(jnp.bfloat16)
                rs_send(way, k, sub, part)

    slot_no = lax.div(y, 4)
    for sub in range(SUBS):
        total = hot_sum[rows_of(z, sub), :]
        for way in range(2):
            total = total + rs_wait(way, 4, sub)[...].astype(jnp.float32)
        part = pl.ds(sub * SUB, SUB)
        partial[part, :] = total.astype(jnp.bfloat16)
        for t, row in enumerate(move_rows):
            @pl.when(row != y)
            def _():
                pltpu.make_async_remote_copy(
                    src_ref=partial.at[part], dst_ref=moved.at[slot_no, part],
                    send_sem=mv_ssem.at[t, sub], recv_sem=mv_rsem.at[slot_no, sub],
                    device_id=device_at(x, row, z, c), device_id_type=MESH,
                ).start()

            @pl.when(row == y)
            def _():
                pltpu.make_async_copy(
                    partial.at[part], moved.at[slot_no, part], mv_rsem.at[slot_no, sub]
                ).start()

    def ag_copy(way, k, sub, piece):
        part = hot_ref.at[rows_of(piece, sub)]
        return pltpu.make_async_remote_copy(
            src_ref=part, dst_ref=part, send_sem=ag_ssem.at[way, k - 1, sub],
            recv_sem=ag_rsem.at[way, k - 1, sub], device_id=z_ids[way], device_id_type=MESH,
        )

    def ag_send(way, k, sub):
        copy = ag_copy(way, k, sub, wrap_z(z + (k - 1 if way == 0 else 1 - k)))
        copy.start()
        pending.append(copy)

    for sub in range(SUBS):
        part = pl.ds(sub * SUB, SUB)
        total = jnp.zeros((SUB, D), jnp.float32)
        for s in range(2):
            pace()
            come = moved.at[s, part]
            pltpu.make_async_copy(come, come, mv_rsem.at[s, sub]).wait()
            total = total + come[...].astype(jnp.float32)
        hot_ref[rows_of(z, sub), :] = total.astype(jnp.bfloat16)
        for way in range(2):
            ag_send(way, 1, sub)
    for k in range(1, 5):
        if k == 4:
            start_cold(COLUMNS)
            loads[3].wait()
            wait_rows(recv_cold, cold_rsem)
            base_ref[...] = outer_sum(recv_cold) + weight * anchor_ref[...].astype(jnp.float32)
        for sub in range(SUBS):
            for way in range(2):
                if k == 4 and sub not in far[way]:
                    continue
                pace()
                ag_copy(way, k, sub, wrap_z(z + (k if way == 0 else -k))).wait_recv()
                if k < 3 or (k == 3 and sub in far[way]):
                    ag_send(way, k + 1, sub)

    wait_rows(send_cold, cold_ssem)
    for copy in pending:
        copy.wait_send()
    for sub in range(SUBS):
        for t, row in enumerate(move_rows):
            @pl.when(row != y)
            def _():
                part = partial.at[pl.ds(sub * SUB, SUB)]
                pltpu.make_async_copy(part, part, mv_ssem.at[t, sub]).wait()


def polar(owned_ref, base_ref, hot_ref, out_ref):
    hot = hot_ref[...].astype(jnp.float32)
    matrix = base_ref[...] + jnp.where(owned_ref[0] > 0, hot, jnp.zeros_like(hot))
    rounded = matrix.astype(jnp.bfloat16)
    last = (((1,), (1,)), ((), ()))
    blocks = [slice(i, i + ROWS) for i in range(0, D, ROWS)]
    gram = [
        lax.dot_general(rounded[rows], rounded, last, preferred_element_type=jnp.float32) for rows in blocks
    ]
    norm = jnp.sqrt(sum(jnp.sum(part * part) for part in gram) + 1e-06)
    iterate = (matrix * (1.0 / jnp.sqrt(norm))).astype(jnp.bfloat16)
    scale = 1.0 / norm
    square = jnp.concatenate([(part * scale).astype(jnp.bfloat16) for part in gram], axis=0)
    for sweep in range(ITERS):
        if sweep > 0:
            square = jnp.concatenate(
                [
                    lax.dot_general(
                        iterate[rows], iterate, last, preferred_element_type=jnp.float32
                    ).astype(jnp.bfloat16)
                    for rows in blocks
                ],
                axis=0,
            )
        made = []
        for rows in blocks:
            twice = jnp.dot(square[rows], square, preferred_element_type=jnp.float32)
            blend = (third_coef * square[rows].astype(jnp.float32) + fifth_coef * twice).astype(jnp.bfloat16)
            update = first_coef * iterate[rows].astype(jnp.float32) + jnp.dot(
                blend, iterate, preferred_element_type=jnp.float32
            )
            if sweep + 1 < ITERS:
                made.append(update.astype(jnp.bfloat16))
            else:
                out_ref[rows, :] = (math.sqrt(D) * update).astype(jnp.bfloat16)
        if made:
            iterate = jnp.concatenate(made, axis=0)


def shards(samples, targets, row_slot, hot_group, anchor):
    rows = samples.shape[0]
    vmem = pl.BlockSpec(memory_space=pltpu.VMEM)
    dma = pltpu.SemaphoreType.DMA
    hbm = pl.BlockSpec(memory_space=pltpu.HBM)
    weight = math.sqrt(D * rows) / 2.0
    hot, base = pl.pallas_call(
        functools.partial(exchange, weight),
        out_shape=(
            jax.ShapeDtypeStruct((D, D), jnp.bfloat16),
            jax.ShapeDtypeStruct((D, D), jnp.float32),
        ),
        in_specs=[hbm] * 4,
        out_specs=(vmem, vmem),
        scratch_shapes=[
            pltpu.VMEM((1, rows), jnp.int32),
            pltpu.VMEM((rows, D), jnp.bfloat16),
            pltpu.VMEM((rows, D), jnp.bfloat16),
            pltpu.VMEM((D, D), jnp.bfloat16),
            pltpu.VMEM((COLUMNS, CAP, 2 * D), jnp.bfloat16),
            pltpu.VMEM((COLUMNS, CAP, 2 * D), jnp.bfloat16),
            pltpu.VMEM((COLUMNS, CAP, 2 * D), jnp.bfloat16),
            pltpu.VMEM((COLUMNS, CAP, 2 * D), jnp.bfloat16),
            pltpu.VMEM((D, D), jnp.float32),
            pltpu.VMEM((2, PIECE // 2, D), jnp.bfloat16),
            pltpu.VMEM((2, PIECE // 2, D), jnp.bfloat16),
            pltpu.VMEM((2, 4, PIECE, D), jnp.bfloat16),
            pltpu.VMEM((PIECE, D), jnp.bfloat16),
            pltpu.VMEM((2, PIECE, D), jnp.bfloat16),
            dma((4,)), dma, dma, dma, dma,
            dma((2, 4, SUBS)), dma((2, 4, SUBS)),
            dma((2, SUBS)), dma((2, SUBS)),
            dma((2, 4, SUBS)), dma((2, 4, SUBS)),
        ],
        compiler_params=pltpu.CompilerParams(
            collective_id=0, has_side_effects=True, vmem_limit_bytes=24 << 20
        ),
    )(*(
        pltpu.with_memory_space_constraint(a, pltpu.HBM)
        for a in (row_slot.reshape(1, rows), samples, targets, anchor[0])
    ))
    owned = (lax.axis_index("grp") == hot_group).astype(jnp.int32)
    rotation = pl.pallas_call(
        polar,
        out_shape=jax.ShapeDtypeStruct((D, D), jnp.bfloat16),
        in_specs=[pl.BlockSpec(memory_space=pltpu.SMEM), vmem, vmem],
        out_specs=vmem,
        compiler_params=pltpu.CompilerParams(vmem_limit_bytes=24 << 20),
    )(owned, base, hot)
    return rotation[None]


def solution(mesh):
    return jax.shard_map(
        shards,
        mesh=mesh,
        in_specs=(
            P(("grp", "dev"), None),
            P(("grp", "dev"), None),
            P(("grp", "dev")),
            P("dev"),
            P(("grp", "dev"), None, None),
        ),
        out_specs=P(("grp", "dev"), None, None),
        check_vma=False,
    )
```

```python
import functools
import math

import jax
import jax.numpy as jnp
from jax import lax
from jax.experimental import pallas as pl
from jax.experimental.pallas import tpu as pltpu
from jax.sharding import PartitionSpec as P

MESH = pl.DeviceIdType.MESH
ITERS = 2
ROWS = 256
first_coef = 3.4445
third_coef = -4.775
fifth_coef = 2.0315

NX, NY, NZ, NC = 4, 8, 8, 2
COLUMNS = 32
CAP = 16
D = 768
PIECE = D // NZ
SUBS = 2
SUB = PIECE // SUBS
FIRST, SECOND, PACE = 0, 6, 1


def device_at(x, y, z, c):
    return (lax.rem(y, 2) * NZ + z, x * 8 + lax.div(y, 2) * 2 + c)


def exchange(
    weight, slot_hbm, samples_hbm, targets_hbm, anchor_hbm, hot_ref, base_ref,
    slot_ref, samples_ref, targets_ref, anchor_ref,
    send_hot, send_cold, recv_hot, recv_cold, hot_sum, rs_first, rs_own, rs_in, partial, moved,
    in_sems, hot_ssem, hot_rsem, cold_ssem, cold_rsem, rs_ssem, rs_rsem, mv_ssem, mv_rsem, ag_ssem, ag_rsem,
):
    grp, dev = lax.axis_index("grp"), lax.axis_index("dev")
    y_lo, z = lax.div(grp, NZ), lax.rem(grp, NZ)
    x, y_hi, c = lax.div(dev, 8), lax.rem(lax.div(dev, 2), 4), lax.rem(dev, 2)
    y = 2 * y_hi + y_lo
    loads = [
        pltpu.make_async_copy(src, dst, in_sems.at[i])
        for i, (src, dst) in enumerate(
            ((slot_hbm, slot_ref), (samples_hbm, samples_ref), (targets_hbm, targets_ref), (anchor_hbm, anchor_ref))
        )
    ]
    for load in loads:
        load.start()
    wrap_x = lambda v: lax.rem(v + NX, NX)
    wrap_y = lambda v: lax.rem(v + NY, NY)
    wrap_z = lambda v: lax.rem(v + NZ, NZ)

    def offsets(r):
        return lax.div(r, 8), lax.rem(lax.div(r, 2), 4), lax.rem(r, 2)

    def gray(v):
        return v + lax.div(v, 2) * (1 - 2 * lax.rem(v, 2))

    def ordered(i):
        u, v = lax.rem(lax.div(i, 4), 4), lax.rem(i, 4)
        return 8 * gray(lax.rem(u + v, 4)) + 2 * gray(v) + lax.div(i, 16)

    def hot_step(q, core):
        return q - 4 * lax.div(2 * q + core, 5)

    def hot_target(r):
        dx, q, dc = offsets(r)
        core = lax.rem(c + dc, 2)
        row = wrap_y(y + hot_step(q, core))
        col = wrap_x(x + dx) * 8 + lax.rem(row, 4) * 2 + core
        return device_at(wrap_x(x + dx), row, z, core), col

    def hot_source(r):
        dx, q, dc = offsets(r)
        return device_at(wrap_x(x - dx), wrap_y(y - hot_step(q, c)), z, lax.rem(c + dc, 2))

    def cold_target(r):
        dx, q, dc = offsets(r)
        core, hi = lax.rem(c + dc, 2), lax.rem(y_hi + q, 4)
        col = wrap_x(x + dx) * 8 + hi * 2 + core
        return (grp, col), col

    def cold_source(r):
        dx, q, dc = offsets(r)
        return (grp, wrap_x(x - dx) * 8 + lax.rem(y_hi + 4 - q, 4) * 2 + lax.rem(c + dc, 2))

    z_ids = (device_at(x, y, wrap_z(z - 1), c), device_at(x, y, wrap_z(z + 1), c))
    move_rows = tuple(2 * lax.rem(y, 4) + t for t in range(2))
    from_rows = tuple(y_hi + 4 * s for s in range(2))

    barrier = pltpu.get_barrier_semaphore()

    def greet(r, carry):
        pl.semaphore_signal(barrier, inc=1, device_id=hot_source(r), device_id_type=MESH)
        pl.semaphore_signal(barrier, inc=1, device_id=cold_source(r), device_id_type=MESH)
        return carry

    lax.fori_loop(1, COLUMNS, greet, 0, unroll=True)
    for other in z_ids:
        pl.semaphore_signal(barrier, inc=1, device_id=other, device_id_type=MESH)
    for row in from_rows:
        @pl.when(row != y)
        def _():
            pl.semaphore_signal(barrier, inc=1, device_id=device_at(x, row, z, c), device_id_type=MESH)

    loads[0].wait()
    slot = slot_ref[...]
    rows = slot.shape[1]
    member = (lax.broadcasted_iota(jnp.int32, (2 * COLUMNS, rows), 0) == slot).astype(jnp.float32)
    before = (
        lax.broadcasted_iota(jnp.int32, (rows, rows), 0) < lax.broadcasted_iota(jnp.int32, (rows, rows), 1)
    ).astype(jnp.float32).astype(jnp.bfloat16)
    count = jnp.dot(member.astype(jnp.bfloat16), before, preferred_element_type=jnp.float32)
    rank = jnp.sum(count * member, axis=0, keepdims=True)
    place = slot * CAP + rank.astype(jnp.int32)

    def sort_into(out, base):
        pick = (
            (lax.broadcasted_iota(jnp.int32, (COLUMNS * CAP, rows), 0) + base) == place
        ).astype(jnp.float32).astype(jnp.bfloat16)
        for ref, lane in ((samples_ref, 0), (targets_ref, D)):
            picked = jnp.dot(pick, ref[...], preferred_element_type=jnp.float32).astype(jnp.bfloat16)
            out[:, :, lane:lane + D] = picked.reshape(COLUMNS, CAP, D)

    loads[1].wait()
    loads[2].wait()
    sort_into(send_hot, COLUMNS * CAP)

    elsewhere = 2 - lax.div(y + 1, NY) - lax.div(NY - y, NY)
    pl.semaphore_wait(barrier, 2 * (COLUMNS - 1) + 2 + elsewhere)

    def send_rows(target, out, into, ssem, rsem, first=1, last=COLUMNS):
        def body(i, carry):
            r = ordered(i)
            where, col = target(r)
            pltpu.make_async_remote_copy(
                src_ref=out.at[col], dst_ref=into.at[r], send_sem=ssem, recv_sem=rsem,
                device_id=where, device_id_type=MESH,
            ).start()
            return carry
        lax.fori_loop(first, last, body, 0, unroll=True)

    def wait_rows(ref, sem):
        many = ref.at[pl.ds(1, COLUMNS - 1)]
        pltpu.make_async_copy(many, many, sem).wait()

    def outer_sum(ref):
        both = ref[...].reshape(COLUMNS * CAP, 2 * D)
        return lax.dot_general(
            both[:, D:], both[:, :D], (((0,), (0,)), ((), ())), preferred_element_type=jnp.float32
        )

    started = [1]
    events = [0]

    def start_cold(n):
        first, last = started[0], min(started[0] + n, COLUMNS)
        if first < last:
            send_rows(cold_target, send_cold, recv_cold, cold_ssem, cold_rsem, first, last)
        started[0] = last

    def pace():
        events[0] += 1
        if events[0] % PACE == 0:
            start_cold(1)

    send_rows(hot_target, send_hot, recv_hot, hot_ssem, hot_rsem)
    recv_hot[0] = send_hot[hot_target(0)[1]]
    sort_into(send_cold, 0)
    recv_cold[0] = send_cold[dev]
    start_cold(FIRST)
    wait_rows(send_hot, hot_ssem)
    start_cold(SECOND)
    wait_rows(recv_hot, hot_rsem)
    hot_sum[...] = outer_sum(recv_hot)

    def rows_of(piece, sub, subs=1):
        return pl.ds(pl.multiple_of(piece * PIECE + sub * SUB, CAP), subs * SUB)

    far = (range(SUBS // 2), range(SUBS // 2, SUBS))
    order = (tuple(far[1]) + tuple(far[0]), tuple(far[0]) + tuple(far[1]))

    def rs_piece(way, k):
        return wrap_z(z + (k - 5 if way == 0 else 5 - k) + NZ)

    def rs_slot(way, k, sub):
        return rs_in.at[way, k - 1, pl.ds(sub * SUB, SUB)]

    def rs_send(way, k, sub, src):
        copy = pltpu.make_async_remote_copy(
            src_ref=src, dst_ref=rs_slot(way, k, sub),
            send_sem=rs_ssem.at[way, k - 1, sub], recv_sem=rs_rsem.at[way, k - 1, sub],
            device_id=z_ids[way], device_id_type=MESH,
        )
        copy.start()
        pending.append(copy)

    def rs_wait(way, k, sub):
        pace()
        part = rs_slot(way, k, sub)
        pltpu.make_async_copy(part, part, rs_rsem.at[way, k - 1, sub]).wait()
        return part

    pending = []
    for k, kept in ((1, rs_first), (2, rs_own)):
        for way in range(2):
            subs = far[way] if k == 1 else far[1 - way]
            kept[way] = hot_sum[rows_of(rs_piece(way, k), subs[0], SUBS // 2), :].astype(jnp.bfloat16)
        for i in range(SUBS // 2):
            for way in range(2):
                subs = far[way] if k == 1 else far[1 - way]
                rs_send(way, k, subs[i], kept.at[way, pl.ds(i * SUB, SUB)])
    for k in range(2, 5):
        for turn in range(SUBS):
            for way in range(2):
                sub = order[way][turn]
                if k == 2 and sub not in far[way]:
                    continue
                part = rs_wait(way, k - 1, sub)
                part[...] = (
                    part[...].astype(jnp.float32) + hot_sum[rows_of(rs_piece(way, k), sub), :]
                ).astype(jnp.bfloat16)
                rs_send(way, k, sub, part)

    slot_no = lax.div(y, 4)
    for sub in range(SUBS):
        total = hot_sum[rows_of(z, sub), :]
        for way in range(2):
            total = total + rs_wait(way, 4, sub)[...].astype(jnp.float32)
        part = pl.ds(sub * SUB, SUB)
        partial[part, :] = total.astype(jnp.bfloat16)
        for t, row in enumerate(move_rows):
            @pl.when(row != y)
            def _():
                pltpu.make_async_remote_copy(
                    src_ref=partial.at[part], dst_ref=moved.at[slot_no, part],
                    send_sem=mv_ssem.at[t, sub], recv_sem=mv_rsem.at[slot_no, sub],
                    device_id=device_at(x, row, z, c), device_id_type=MESH,
                ).start()

            @pl.when(row == y)
            def _():
                pltpu.make_async_copy(
                    partial.at[part], moved.at[slot_no, part], mv_rsem.at[slot_no, sub]
                ).start()

    def ag_copy(way, k, sub, piece):
        part = hot_ref.at[rows_of(piece, sub)]
        return pltpu.make_async_remote_copy(
            src_ref=part, dst_ref=part, send_sem=ag_ssem.at[way, k - 1, sub],
            recv_sem=ag_rsem.at[way, k - 1, sub], device_id=z_ids[way], device_id_type=MESH,
        )

    def ag_send(way, k, sub):
        copy = ag_copy(way, k, sub, wrap_z(z + (k - 1 if way == 0 else 1 - k)))
        copy.start()
        pending.append(copy)

    for sub in range(SUBS):
        part = pl.ds(sub * SUB, SUB)
        total = jnp.zeros((SUB, D), jnp.float32)
        for s in range(2):
            pace()
            come = moved.at[s, part]
            pltpu.make_async_copy(come, come, mv_rsem.at[s, sub]).wait()
            total = total + come[...].astype(jnp.float32)
        hot_ref[rows_of(z, sub), :] = total.astype(jnp.bfloat16)
        for way in range(2):
            ag_send(way, 1, sub)
    for k in range(1, 5):
        if k == 4:
            start_cold(COLUMNS)
            loads[3].wait()
            wait_rows(recv_cold, cold_rsem)
            base_ref[...] = outer_sum(recv_cold) + weight * anchor_ref[...].astype(jnp.float32)
        for sub in range(SUBS):
            for way in range(2):
                if k == 4 and sub not in far[way]:
                    continue
                pace()
                ag_copy(way, k, sub, wrap_z(z + (k if way == 0 else -k))).wait_recv()
                if k < 3 or (k == 3 and sub in far[way]):
                    ag_send(way, k + 1, sub)

    wait_rows(send_cold, cold_ssem)
    for copy in pending:
        copy.wait_send()
    for sub in range(SUBS):
        for t, row in enumerate(move_rows):
            @pl.when(row != y)
            def _():
                part = partial.at[pl.ds(sub * SUB, SUB)]
                pltpu.make_async_copy(part, part, mv_ssem.at[t, sub]).wait()


def polar(owned_ref, base_ref, hot_ref, out_ref):
    hot = hot_ref[...].astype(jnp.float32)
    matrix = base_ref[...] + jnp.where(owned_ref[0] > 0, hot, jnp.zeros_like(hot))
    rounded = matrix.astype(jnp.bfloat16)
    last = (((1,), (1,)), ((), ()))
    blocks = [slice(i, i + ROWS) for i in range(0, D, ROWS)]
    gram = [
        lax.dot_general(rounded[rows], rounded, last, preferred_element_type=jnp.float32) for rows in blocks
    ]
    norm = jnp.sqrt(sum(jnp.sum(part * part) for part in gram) + 1e-06)
    iterate = (matrix * (1.0 / jnp.sqrt(norm))).astype(jnp.bfloat16)
    scale = 1.0 / norm
    square = jnp.concatenate([(part * scale).astype(jnp.bfloat16) for part in gram], axis=0)
    for sweep in range(ITERS):
        if sweep > 0:
            square = jnp.concatenate(
                [
                    lax.dot_general(
                        iterate[rows], iterate, last, preferred_element_type=jnp.float32
                    ).astype(jnp.bfloat16)
                    for rows in blocks
                ],
                axis=0,
            )
        made = []
        for rows in blocks:
            twice = jnp.dot(square[rows], square, preferred_element_type=jnp.float32)
            blend = (third_coef * square[rows].astype(jnp.float32) + fifth_coef * twice).astype(jnp.bfloat16)
            update = first_coef * iterate[rows].astype(jnp.float32) + jnp.dot(
                blend, iterate, preferred_element_type=jnp.float32
            )
            if sweep + 1 < ITERS:
                made.append(update.astype(jnp.bfloat16))
            else:
                out_ref[rows, :] = (math.sqrt(D) * update).astype(jnp.bfloat16)
        if made:
            iterate = jnp.concatenate(made, axis=0)


def shards(samples, targets, row_slot, hot_group, anchor):
    rows = samples.shape[0]
    vmem = pl.BlockSpec(memory_space=pltpu.VMEM)
    dma = pltpu.SemaphoreType.DMA
    hbm = pl.BlockSpec(memory_space=pltpu.HBM)
    weight = math.sqrt(D * rows) / 2.0
    hot, base = pl.pallas_call(
        functools.partial(exchange, weight),
        out_shape=(
            jax.ShapeDtypeStruct((D, D), jnp.bfloat16),
            jax.ShapeDtypeStruct((D, D), jnp.float32),
        ),
        in_specs=[hbm] * 4,
        out_specs=(vmem, vmem),
        scratch_shapes=[
            pltpu.VMEM((1, rows), jnp.int32),
            pltpu.VMEM((rows, D), jnp.bfloat16),
            pltpu.VMEM((rows, D), jnp.bfloat16),
            pltpu.VMEM((D, D), jnp.bfloat16),
            pltpu.VMEM((COLUMNS, CAP, 2 * D), jnp.bfloat16),
            pltpu.VMEM((COLUMNS, CAP, 2 * D), jnp.bfloat16),
            pltpu.VMEM((COLUMNS, CAP, 2 * D), jnp.bfloat16),
            pltpu.VMEM((COLUMNS, CAP, 2 * D), jnp.bfloat16),
            pltpu.VMEM((D, D), jnp.float32),
            pltpu.VMEM((2, PIECE // 2, D), jnp.bfloat16),
            pltpu.VMEM((2, PIECE // 2, D), jnp.bfloat16),
            pltpu.VMEM((2, 4, PIECE, D), jnp.bfloat16),
            pltpu.VMEM((PIECE, D), jnp.bfloat16),
            pltpu.VMEM((2, PIECE, D), jnp.bfloat16),
            dma((4,)), dma, dma, dma, dma,
            dma((2, 4, SUBS)), dma((2, 4, SUBS)),
            dma((2, SUBS)), dma((2, SUBS)),
            dma((2, 4, SUBS)), dma((2, 4, SUBS)),
        ],
        compiler_params=pltpu.CompilerParams(
            collective_id=0, has_side_effects=True, vmem_limit_bytes=24 << 20
        ),
    )(*(
        pltpu.with_memory_space_constraint(a, pltpu.HBM)
        for a in (row_slot.reshape(1, rows), samples, targets, anchor[0])
    ))
    owned = (lax.axis_index("grp") == hot_group).astype(jnp.int32)
    rotation = pl.pallas_call(
        polar,
        out_shape=jax.ShapeDtypeStruct((D, D), jnp.bfloat16),
        in_specs=[pl.BlockSpec(memory_space=pltpu.SMEM), vmem, vmem],
        out_specs=vmem,
        compiler_params=pltpu.CompilerParams(vmem_limit_bytes=24 << 20),
    )(owned, base, hot)
    return rotation[None]


def solution(mesh):
    return jax.shard_map(
        shards,
        mesh=mesh,
        in_specs=(
            P(("grp", "dev"), None),
            P(("grp", "dev"), None),
            P(("grp", "dev")),
            P("dev"),
            P(("grp", "dev"), None, None),
        ),
        out_specs=P(("grp", "dev"), None, None),
        check_vma=False,
    )
```
